32 devices in a mesh: rep: 2 (over x), seq: 16 (over z, y, core).
Axes of the slice: x: 2, y: 2, z: 4, core: 2. Of those that a mesh axis runs over, the one named last changes fastest.
Arguments:
- qkv: bfloat16 [4096, 40, 3, 128], P(('rep', 'seq')), parts along dimension 0, may hold values from -10 to 10, as said below
- block_ids: int32 [32, 40, 4], P(('rep', 'seq')), parts along dimension 0, may hold values from 0 to 15, as said below
- counts: int32 [32, 40], P(('rep', 'seq')), parts along dimension 0, may hold values from 1 to 4, as said below
Outputs:
- attended: bfloat16 [4096, 40, 128], P(('rep', 'seq')), parts along dimension 0
The draws below stay inside these ranges and needn't reach their ends.
There are 2 independent parts, one for each index of `rep`. The reference program is written for one: setup_inputs(seed, part) draws one part's arguments, and reference() takes and returns one part's arrays. A program takes and returns all parts, laid end to end along the dimension named above; each array names one. Nothing has to cross between parts.
Inputs may be any that keep to these rules, and one draw needn't show every extreme that they name: `qkv`: real values; a few queries may nearly coincide with scaled keys of their own block. `block_ids`: the entries of one list are distinct, and entry 0 is the query block itself. Entries at positions counts and beyond are padding and are ignored. Live counts vary from head to head; the most, 4, is reached in every draw.
All inputs are finite; a program needn't handle non-finite values.
Results may differ from the reference program's by a relative error of at most 0.0044.
Values may be sent and summed in bfloat16 or wider, within the bound.
No kernel may reach another device: no remote copies, remote signals or barrier semaphores. Data moves between devices by JAX's collectives and lax.ppermute only.
A program may use at most 128 MiB of HBM per device.

```python
import math
import jax
import jax.numpy as jnp
from jax import lax

HEADS = 40
HEAD_DIM = 128
BLOCK = 128
NB = 4
TOKENS = 2048
QB = 16


def draw_qkv(key, part):
    key = jax.random.fold_in(key, 11)
    first = jax.random.fold_in(key, 0)
    shape = (TOKENS, HEADS, 3, HEAD_DIM)
    values = jnp.clip(jax.random.normal(first, shape, jnp.float32), -4.0, 4.0)
    return values.astype(jnp.bfloat16)


def draw_block_ids(key, part):
    key = jax.random.fold_in(key, 23)
    raw = jax.random.randint(key, (QB, HEADS, QB - 1), 0, 1 << 20, dtype=jnp.int32)
    distinct = raw * QB + jnp.arange(QB - 1, dtype=jnp.int32)
    unused, offsets = lax.top_k(distinct, NB - 1)
    own = jnp.arange(QB, dtype=jnp.int32)[:, None, None]
    others = (own + offsets.astype(jnp.int32) + 1) % QB
    return jnp.concatenate([jnp.broadcast_to(own, (QB, HEADS, 1)), others], axis=2).astype(jnp.int32)


def draw_counts(key, part):
    key = jax.random.fold_in(key, 37)
    first, second, third = jax.random.split(key, 3)
    level = jax.random.randint(first, (HEADS,), 1, NB + 1, dtype=jnp.int32)
    heaviest = jax.random.randint(second, (), 0, HEADS, dtype=jnp.int32)
    level = jnp.where(jnp.arange(HEADS, dtype=jnp.int32) == heaviest, NB, level)
    lowered = jax.random.randint(third, (QB, HEADS), 0, 2, dtype=jnp.int32)
    result = jnp.maximum(level[None, :] - lowered, 1)
    result = result.at[0, heaviest].set(NB)
    return result.astype(jnp.int32)


def setup_inputs(seed: int = 0, part: int = 0) -> dict:
    seeds = jax.random.split(jax.random.key(seed), 4)
    part_keys = jax.random.split(jax.random.fold_in(seeds[3], part), 4)
    qkv = draw_qkv(jax.random.fold_in(jax.random.fold_in(seeds[3], part), 71), part)
    block_ids = draw_block_ids(jax.random.fold_in(jax.random.fold_in(seeds[3], part), 71), part)
    counts = draw_counts(jax.random.fold_in(jax.random.fold_in(seeds[3], part), 71), part)
    return dict(qkv=qkv, block_ids=block_ids, counts=counts)


def one_head(inputs):
    rows, key_ids, live_count = inputs
    blocks = rows.reshape(QB, BLOCK, 3, HEAD_DIM)
    queries = blocks[:, :, 0].astype(jnp.float32)
    key_blocks = blocks[:, :, 1][key_ids].astype(jnp.float32)
    value_blocks = blocks[:, :, 2][key_ids].astype(jnp.float32)
    scores = jnp.einsum('qid,qnjd->qinj', queries, key_blocks) / math.sqrt(HEAD_DIM)
    is_live = (jnp.arange(NB, dtype=jnp.int32)[None, :] < live_count[:, None])[:, None, :, None]
    peak = lax.optimization_barrier(jnp.max(jnp.where(is_live, scores, -jnp.inf), axis=(2, 3), keepdims=True))
    weights = jnp.where(is_live, jnp.exp(scores - peak), 0.0)
    total = lax.optimization_barrier(jnp.sum(weights, axis=(2, 3)))
    rounded = lax.optimization_barrier(weights.astype(jnp.bfloat16)).astype(jnp.float32)
    mixed = jnp.einsum('qinj,qnjd->qid', rounded, value_blocks)
    return (mixed / total[..., None]).astype(jnp.bfloat16).reshape(TOKENS, HEAD_DIM)

def reference(qkv, block_ids, counts):
    per_head = lax.map(one_head, (jnp.moveaxis(qkv, 1, 0), jnp.moveaxis(block_ids, 1, 0), counts.T))
    return jnp.moveaxis(per_head, 0, 1)
```

```python
import functools
import math

import jax
import jax.numpy as jnp
from jax import lax
from jax.experimental import pallas as pl
from jax.experimental.pallas import tpu as pltpu
from jax.sharding import PartitionSpec as P

F32, BF16 = jnp.float32, jnp.bfloat16
DEAD = -1e30
VMEM_BYTES = 48 << 20


def params(cost=None):
    return pltpu.CompilerParams(vmem_limit_bytes=VMEM_BYTES)


def slots(heads, per_chip, chips):
    even = per_chip // 2
    whole, shared = [], []
    for head in range(heads):
        chip, inner = divmod(head, per_chip)
        if inner < 2 * even:
            whole.append((head, 2 * chip + inner // even, inner % even))
        else:
            shared.append((head, 2 * chip))
    return whole, shared


def pack_kernel(whole, shared, even, x_ref, out_ref, wide):
    rows, _, heads, dim = x_ref.shape

    def widen(t, carry):
        wide[pl.ds(pl.multiple_of(t * heads, 8), heads), :] = x_ref[t, 0].astype(F32)
        return carry

    lax.fori_loop(0, rows, widen, 0, unroll=8)
    half = rows // 2
    for head, device, slot in whole:
        out_ref[device, 0, slot * rows : (slot + 1) * rows, :] = wide[
            pl.ds(head, rows, stride=heads), :
        ].astype(BF16)
    for head, device in shared:
        for core in range(2):
            out_ref[device + core, 0, even * rows : even * rows + half, :] = wide[
                pl.ds(core * half * heads + head, half, stride=heads), :
            ].astype(BF16)


def unpack_kernel(whole, shared, even, x_ref, out_ref, wide):
    rows, heads, dim = out_ref.shape
    half = rows // 2
    for head, device, slot in whole:
        wide[pl.ds(head, rows, stride=heads), :] = x_ref[
            device, slot * rows : (slot + 1) * rows, :
        ].astype(F32)
    for head, device in shared:
        for core in range(2):
            wide[pl.ds(core * half * heads + head, half, stride=heads), :] = x_ref[
                device + core, even * rows : even * rows + half, :
            ].astype(F32)

    def narrow(t, carry):
        out_ref[t] = wide[pl.ds(pl.multiple_of(t * heads, 8), heads), :].astype(BF16)
        return carry

    lax.fori_loop(0, rows, narrow, 0, unroll=8)


def attend_block(queries, keys, values, count, scale):
    picked = jnp.concatenate(keys, axis=0)
    scores = lax.dot_general(
        queries, picked, (((1,), (1,)), ((), ())), preferred_element_type=F32
    )
    width = keys[0].shape[0]
    parts = []
    for j in range(len(keys)):
        part = scores[:, j * width : (j + 1) * width] * scale
        if j:
            part = part + jnp.where(j < count, 0.0, DEAD).astype(F32)
        parts.append(part)
    peak = functools.reduce(jnp.maximum, parts)
    peak = jnp.max(peak, axis=1, keepdims=True)
    weights = [jnp.exp2(part - peak) for part in parts]
    total = jnp.sum(functools.reduce(jnp.add, weights), axis=1, keepdims=True)
    rounded = jnp.concatenate([w.astype(BF16) for w in weights], axis=1)
    mixed = jnp.dot(rounded, jnp.concatenate(values, axis=0), preferred_element_type=F32)
    return (mixed / total).astype(BF16)


def whole_kernel(lists, heads, scale, info_ref, owned_ref, x_ref, out_ref):
    blocks = x_ref.shape[0]
    head = owned_ref[pl.program_id(0)]

    def one(b, carry):
        base = (b * heads + head) * (lists + 1)
        ids = [info_ref[base + j] for j in range(lists)]
        out_ref[b] = attend_block(
            x_ref[b, 0],
            [x_ref[c, 1] for c in ids],
            [x_ref[c, 2] for c in ids],
            info_ref[base + lists],
            scale,
        )
        return carry

    lax.fori_loop(0, blocks, one, 0, unroll=2)


def shared_kernel(lists, heads, scale, info_ref, owned_ref, x_ref, far_ref, held_ref, out_ref):
    blocks = x_ref.shape[0]
    head = owned_ref[0]

    def one(b, carry):
        base = (b * heads + head) * (lists + 1)
        ids = [info_ref[base + j] for j in range(lists)]
        keys, values = [], []
        for c in ids:
            keys.append(jnp.concatenate([x_ref[c, 1], far_ref[c, 0]], axis=0))
            values.append(jnp.concatenate([x_ref[c, 2], far_ref[c, 1]], axis=0))
        out_ref[b] = attend_block(x_ref[b, 0], keys, values, info_ref[base + lists], scale)
        return carry

    lax.fori_loop(0, blocks, one, 0, unroll=2)


def body(seq, qkv, block_ids, counts):
    rows, heads, _, dim = qkv.shape
    lists = block_ids.shape[2]
    chips = seq // 2
    per_chip = -(-heads // chips)
    even, odd = divmod(per_chip, 2)
    half = rows // 2
    depth = even * rows + odd * half
    whole, shared = slots(heads, per_chip, chips)
    scale = math.log2(math.e) / math.sqrt(dim)

    info = jnp.concatenate([block_ids, counts[:, :, None]], axis=2).reshape(1, -1)
    info = lax.all_gather(info, "seq", axis=0, tiled=True).reshape(-1)

    by_kind = jnp.transpose(qkv, (0, 2, 1, 3))
    sent = pl.pallas_call(
        functools.partial(pack_kernel, whole, shared, even),
        grid=(3,),
        in_specs=[pl.BlockSpec((rows, 1, heads, dim), lambda s: (0, s, 0, 0))],
        out_specs=pl.BlockSpec((seq, 1, depth, dim), lambda s: (0, s, 0, 0)),
        out_shape=jax.ShapeDtypeStruct((seq, 3, depth, dim), BF16),
        scratch_shapes=[pltpu.VMEM((rows * heads, dim), F32)],
        compiler_params=params(),
        name="pack",
    )(by_kind)
    came = lax.all_to_all(sent, "seq", split_axis=0, concat_axis=0, tiled=True)

    me = lax.axis_index("seq")
    first = me // 2 * per_chip
    owned = first + me % 2 * even + jnp.arange(even, dtype=jnp.int32)
    owned = jnp.minimum(owned, heads - 1)
    result = pl.pallas_call(
        functools.partial(whole_kernel, lists, heads, scale),
        grid_spec=pltpu.PrefetchScalarGridSpec(
            num_scalar_prefetch=2,
            grid=(even,),
            in_specs=[pl.BlockSpec((seq, 3, rows, dim), lambda e, *_: (0, 0, e, 0))],
            out_specs=pl.BlockSpec((seq, rows, dim), lambda e, *_: (0, e, 0)),
        ),
        out_shape=jax.ShapeDtypeStruct((seq, depth, dim), BF16),
        compiler_params=params(),
        name="attend_whole",
    )(info, owned, came)
    if odd:
        mine = came[:, 1:, even * rows :, :]
        pairs = [(d, d ^ 1) for d in range(seq)]
        far = lax.ppermute(mine, "seq", pairs)
        owned = jnp.minimum(first + 2 * even, heads - 1).reshape(1)
        result = pl.pallas_call(
            functools.partial(shared_kernel, lists, heads, scale),
            grid_spec=pltpu.PrefetchScalarGridSpec(
                num_scalar_prefetch=2,
                grid=(1,),
                in_specs=[
                    pl.BlockSpec((seq, 3, half, dim), lambda e, *_: (0, 0, 2 * even, 0)),
                    pl.BlockSpec((seq, 2, half, dim), lambda e, *_: (0, 0, 0, 0)),
                    pl.BlockSpec(memory_space=pl.ANY),
                ],
                out_specs=pl.BlockSpec((seq, half, dim), lambda e, *_: (0, 2 * even, 0)),
            ),
            out_shape=jax.ShapeDtypeStruct((seq, depth, dim), BF16),
            input_output_aliases={4: 0},
            compiler_params=params(),
            name="attend_shared",
        )(info, owned, came, far, result)

    back = lax.all_to_all(result, "seq", split_axis=0, concat_axis=0, tiled=True)
    return pl.pallas_call(
        functools.partial(unpack_kernel, whole, shared, even),
        out_shape=jax.ShapeDtypeStruct((rows, heads, dim), BF16),
        scratch_shapes=[pltpu.VMEM((rows * heads, dim), F32)],
        compiler_params=params(),
        name="unpack",
    )(back)


def solution(mesh):
    in_specs = (
        P(("rep", "seq"), None, None, None),
        P(("rep", "seq"), None, None),
        P(("rep", "seq"), None),
    )
    out_specs = P(("rep", "seq"), None, None)
    return jax.shard_map(
        functools.partial(body, mesh.shape["seq"]),
        mesh=mesh,
        in_specs=in_specs,
        out_specs=out_specs,
        check_vma=False,
    )
```

```python
import functools
import math

import jax
import jax.numpy as jnp
from jax import lax
from jax.experimental import pallas as pl
from jax.experimental.pallas import tpu as pltpu
from jax.sharding import PartitionSpec as P

F32, BF16, I32 = jnp.float32, jnp.bfloat16, jnp.int32
DEAD = -1e30
VMEM_BYTES = 48 << 20
INFO_ROWS = 16
GROUP = 4
WINDOW = 6
LATE = 4


def params():
    return pltpu.CompilerParams(vmem_limit_bytes=VMEM_BYTES)


def cost(flops, count):
    return pl.CostEstimate(flops=flops, bytes_accessed=count, transcendentals=0)


class Piece:
    def __init__(self, seq, heads, rows, dim, lists, blocks, first, size):
        self.seq, self.heads, self.rows, self.dim = seq, heads, rows, dim
        self.chips = seq // 2
        self.per_chip = -(-heads // self.chips)
        self.padded = self.per_chip * self.chips > heads
        self.lists, self.first, self.size = lists, first, size
        self.depth = size * rows
        self.bits = max(1, (blocks - 1).bit_length())
        assert self.chips & (self.chips - 1) == 0
        assert lists * self.bits + lists.bit_length() < 31 and lists < INFO_ROWS

    def head(self, chip, slot):
        return chip * self.per_chip + self.first + slot


def pack_kernel(piece, me_ref, x_ref, ids_ref, counts_ref, *refs):
    outs, (wide, info) = refs[: piece.chips], refs[piece.chips :]
    rows, _, heads, _ = x_ref.shape
    chip = me_ref[0] // 2

    def widen(t, carry):
        wide[pl.ds(pl.multiple_of(t * heads, 8), heads), :] = x_ref[t, 0].astype(F32)
        return carry

    lax.fori_loop(0, rows, widen, 0, unroll=8)
    info[...] = jnp.zeros_like(info)
    info[: piece.lists, :heads] = ids_ref[0].astype(F32)
    info[piece.lists : piece.lists + 1, :heads] = counts_ref[...].astype(F32)
    for step, out in enumerate(outs):
        for slot in range(piece.size):
            head = jnp.minimum(piece.head(chip ^ step, slot), heads - 1)
            out[0, slot * rows : (slot + 1) * rows, :] = wide[
                pl.ds(head, rows, stride=heads), :
            ].astype(BF16)
        out[0, piece.depth :, :] = info[...].astype(BF16)


def pack(piece, me, by_kind, block_ids, counts):
    rows, kinds, heads, dim = by_kind.shape
    depth = piece.depth + INFO_ROWS
    return pl.pallas_call(
        functools.partial(pack_kernel, piece),
        grid_spec=pltpu.PrefetchScalarGridSpec(
            num_scalar_prefetch=1,
            grid=(kinds,),
            in_specs=[
                pl.BlockSpec((rows, 1, heads, dim), lambda s, *_: (0, s, 0, 0)),
                pl.BlockSpec((1, piece.lists, heads), lambda s, *_: (0, 0, 0)),
                pl.BlockSpec((1, heads), lambda s, *_: (0, 0)),
            ],
            out_specs=[pl.BlockSpec((1, depth, dim), lambda s, *_: (s, 0, 0))] * piece.chips,
            scratch_shapes=[
                pltpu.VMEM((rows * heads, dim), F32),
                pltpu.VMEM((INFO_ROWS, dim), F32),
            ],
        ),
        out_shape=[jax.ShapeDtypeStruct((kinds, depth, dim), BF16)] * piece.chips,
        compiler_params=params(),
        cost_estimate=cost(0, 8 << 20),
        name="pack",
    )(me, by_kind, jnp.transpose(block_ids, (0, 2, 1)), counts)


def gather_kernel(piece, *refs):
    rows_refs, out_ref, sem = refs[:-2], refs[-2], refs[-1]
    copies = [
        pltpu.make_async_copy(ref.at[1:3, : piece.depth], out_ref.at[step], sem.at[step])
        for step, ref in enumerate(rows_refs)
    ]
    for copy in copies:
        copy.start()
    for copy in copies:
        copy.wait()


def gather_keys(piece, came):
    return pl.pallas_call(
        functools.partial(gather_kernel, piece),
        in_specs=[pl.BlockSpec(memory_space=pl.ANY)] * piece.chips,
        out_specs=pl.BlockSpec(memory_space=pl.ANY),
        out_shape=jax.ShapeDtypeStruct((piece.chips, 2, piece.depth, piece.dim), BF16),
        scratch_shapes=[pltpu.SemaphoreType.DMA((piece.chips,))],
        compiler_params=params(),
        cost_estimate=cost(0, 4 << 20),
        name="gather_keys",
    )(*came)


def attend_group(units, scale):
    scores = [
        lax.dot_general(q, k, (((1,), (1,)), ((), ())), preferred_element_type=F32)
        for q, k, _, _ in units
    ]
    scores = [s * scale + bias for s, (_, _, _, bias) in zip(scores, units)]
    peaks = [jnp.max(s, axis=1, keepdims=True) for s in scores]
    weights = [jnp.exp2(s - peak) for s, peak in zip(scores, peaks)]
    totals = [jnp.sum(w, axis=1, keepdims=True) for w in weights]
    mixed = [
        jnp.dot(w.astype(BF16), v, preferred_element_type=F32)
        for w, (_, _, v, _) in zip(weights, units)
    ]
    return [(m / t).astype(BF16) for m, t in zip(mixed, totals)]


def attend_kernel(piece, scale, me_ref, *refs):
    chips, rows, lists, bits = piece.chips, piece.rows, piece.lists, piece.bits
    near, far_ref, outs = refs[:chips], refs[chips], refs[chips + 1 : 2 * chips + 1]
    queries, keys, values, info, bias, code, scalars, sem = refs[2 * chips + 1 :]
    chip, core = me_ref[0] // 2, me_ref[0] % 2

    copies = []
    for step, ref in enumerate(near):
        inside = slice(0, piece.depth)
        moves = [
            (ref.at[0, piece.depth :], info.at[step]),
            (ref.at[0, inside], queries.at[step]),
            (ref.at[1, inside], keys.at[2 * step]),
            (ref.at[2, inside], values.at[2 * step]),
            (far_ref.at[step, 0], keys.at[2 * step + 1]),
            (far_ref.at[step, 1], values.at[2 * step + 1]),
        ]
        copies += [
            pltpu.make_async_copy(source, target, sem.at[step, at])
            for at, (source, target) in enumerate(moves)
        ]
    for copy in copies:
        copy.start()

    width = lists * rows
    count = lax.broadcasted_iota(I32, bias.shape, 0)
    entry = lax.broadcasted_iota(I32, bias.shape, 1) // rows
    bias[...] = jnp.where((entry < count) | (entry == 0), 0.0, DEAD).astype(F32)
    for copy in copies:
        copy.wait()

    for step in range(chips):
        row = info[step].astype(F32).astype(I32)
        total = row[:1]
        for j in range(1, lists + 1):
            total = total + (row[j : j + 1] << (j * bits))
        code[step : step + 1, :] = total
    copy = pltpu.make_async_copy(code, scalars, sem.at[0, 0])
    copy.start()
    copy.wait()

    mask = (1 << bits) - 1

    def place(block):
        return ((block // 2) ^ chip) * 2 + ((block % 2) ^ core)

    def one_slot(slot, carry):
        head = jnp.minimum(piece.head(chip, slot), piece.heads - 1)
        span = pl.ds(pl.multiple_of(slot * rows, rows), rows)
        for start in range(0, chips, GROUP):
            steps, units = range(start, min(start + GROUP, chips)), []
            for step in steps:
                number = scalars[step, head]
                places = [place((number >> (j * bits)) & mask) for j in range(lists)]
                live = number >> (lists * bits)
                units.append(
                    (
                        queries[step, span, :],
                        jnp.concatenate([keys[c, span, :] for c in places], axis=0),
                        jnp.concatenate([values[c, span, :] for c in places], axis=0),
                        bias[pl.ds(live, 1), :],
                    )
                )
            for step, result in zip(steps, attend_group(units, scale)):
                outs[step][span, :] = result
        return carry

    lax.fori_loop(0, piece.size, one_slot, 0)


def attend(piece, me, came, far, scale):
    chips, depth, dim = piece.chips, piece.depth, piece.dim
    bias_rows = -(-(piece.lists + 1) // 8) * 8
    any_spec = pl.BlockSpec(memory_space=pl.ANY)
    return pl.pallas_call(
        functools.partial(attend_kernel, piece, scale),
        in_specs=[pl.BlockSpec(memory_space=pltpu.SMEM)] + [any_spec] * (chips + 1),
        out_specs=[pl.BlockSpec(memory_space=pltpu.VMEM)] * chips,
        out_shape=[jax.ShapeDtypeStruct((depth, dim), BF16)] * chips,
        scratch_shapes=[
            pltpu.VMEM((chips, depth, dim), BF16),
            pltpu.VMEM((2 * chips, depth, dim), BF16),
            pltpu.VMEM((2 * chips, depth, dim), BF16),
            pltpu.VMEM((chips, INFO_ROWS, dim), BF16),
            pltpu.VMEM((bias_rows, piece.lists * piece.rows), F32),
            pltpu.VMEM((chips, dim), I32),
            pltpu.SMEM((chips, dim), I32),
            pltpu.SemaphoreType.DMA((chips, 6)),
        ],
        compiler_params=params(),
        cost_estimate=cost(4 << 30, 8 << 20),
        name="attend",
    )(me, *came, far)


def unpack_kernel(pieces, me_ref, *refs):
    backs, (out_ref, wide) = refs[:-2], refs[-2:]
    rows, heads, _ = out_ref.shape
    chip, at = me_ref[0] // 2, 0
    for piece in pieces:
        for step in range(piece.chips):
            for slot in range(piece.size):
                head = piece.head(chip ^ step, slot)

                def spread(ref=backs[at], head=head, slot=slot):
                    wide[pl.ds(head, rows, stride=heads), :] = ref[
                        slot * rows : (slot + 1) * rows, :
                    ].astype(F32)

                if piece.padded:
                    pl.when(head < heads)(spread)
                else:
                    spread()
            at += 1

    def narrow(t, carry):
        out_ref[t] = wide[pl.ds(pl.multiple_of(t * heads, 8), heads), :].astype(BF16)
        return carry

    lax.fori_loop(0, rows, narrow, 0, unroll=8)


def unpack(pieces, me, backs):
    first = pieces[0]
    rows, heads, dim = first.rows, first.heads, first.dim
    flat = [back for group in backs for back in group]
    return pl.pallas_call(
        functools.partial(unpack_kernel, pieces),
        in_specs=[pl.BlockSpec(memory_space=pltpu.SMEM)]
        + [pl.BlockSpec(memory_space=pltpu.VMEM)] * len(flat),
        out_specs=pl.BlockSpec(memory_space=pltpu.VMEM),
        out_shape=jax.ShapeDtypeStruct((rows, heads, dim), BF16),
        scratch_shapes=[pltpu.VMEM((rows * heads, dim), F32)],
        compiler_params=params(),
        cost_estimate=cost(0, 4 << 20),
        name="unpack",
    )(me, *flat)


def order_of(chips):
    far = list(range(chips // 2, chips))
    near = list(range(1, chips // 2))
    mixed = [step for pair in zip(far, near) for step in pair]
    return mixed + far[len(near) :]


class Sender:
    def __init__(self, seq):
        self.seq, self.ended = seq, []

    def exchange(self, arrays, after=None, late=None):
        got = list(arrays)
        for at, m in enumerate(order_of(self.seq // 2)):
            a = arrays[m]
            if after is not None and at == late:
                a, _ = lax.optimization_barrier((a, after))
            if len(self.ended) >= WINDOW:
                a, _ = lax.optimization_barrier((a, self.ended[-WINDOW]))
            got[m] = lax.ppermute(a, "seq", [(d, d ^ (2 * m)) for d in range(self.seq)])
            self.ended.append(got[m])
        return got


def body(seq, qkv, block_ids, counts):
    rows, heads, _, dim = qkv.shape
    per_chip = -(-heads // (seq // 2))
    make = functools.partial(
        Piece, seq, heads, rows, dim, block_ids.shape[2], seq * block_ids.shape[0]
    )
    cut = -(-per_chip * 3 // 5)
    pieces = [make(0, cut)] + ([make(cut, per_chip - cut)] if cut < per_chip else [])
    scale = math.log2(math.e) / math.sqrt(dim)
    me = lax.axis_index("seq").astype(I32).reshape(1)
    by_kind = jnp.transpose(qkv, (0, 2, 1, 3))

    packed = [pack(piece, me, by_kind, block_ids, counts) for piece in pieces]
    sender, outs, backs, after = Sender(seq), [], [], packed[-1][0]
    for piece, rows_of in zip(pieces, packed):
        rows_of = sender.exchange(rows_of, after, WINDOW)
        mine = gather_keys(piece, rows_of)
        far = lax.ppermute(mine, "seq", [(d, d ^ 1) for d in range(seq)])
        outs.append(attend(piece, me, rows_of, far, scale))
        after = outs[-1][0]
    backs = [sender.exchange(out, outs[-1][0], LATE) for out in outs]
    return unpack(pieces, me, backs)


def solution(mesh):
    in_specs = (
        P(("rep", "seq"), None, None, None),
        P(("rep", "seq"), None, None),
        P(("rep", "seq"), None),
    )
    out_specs = P(("rep", "seq"), None, None)
    return jax.shard_map(
        functools.partial(body, mesh.shape["seq"]),
        mesh=mesh,
        in_specs=in_specs,
        out_specs=out_specs,
        check_vma=False,
    )
```

```python
import functools
import math

import jax
import jax.numpy as jnp
from jax import lax
from jax.experimental import pallas as pl
from jax.experimental.pallas import tpu as pltpu
from jax.sharding import PartitionSpec as P

F32, BF16, I32 = jnp.float32, jnp.bfloat16, jnp.int32
DEAD = -1e30
VMEM_BYTES = 48 << 20
PACK_BYTES = 60 << 20
MIX_BACK = True
INFO_ROWS = 16
GROUP = 4
WINDOW = 8
LATE_A = 3
SEEN_A = 0
LATE_B = 3
SEEN_B = 2


def params(limit=VMEM_BYTES):
    return pltpu.CompilerParams(vmem_limit_bytes=limit)


def cost(flops, count):
    return pl.CostEstimate(flops=flops, bytes_accessed=count, transcendentals=0)


class Plan:
    def __init__(self, seq, heads, rows, dim, lists, blocks):
        self.seq, self.heads, self.rows, self.dim, self.lists = seq, heads, rows, dim, lists
        self.chips = seq // 2
        self.per_chip = -(-heads // self.chips)
        self.padded = self.per_chip * self.chips > heads
        self.bits = max(1, (blocks - 1).bit_length())
        assert self.chips & (self.chips - 1) == 0
        assert lists * self.bits + lists.bit_length() < 31 and lists < INFO_ROWS
        self.near = list(range(max(1, self.chips // 2)))
        self.far = list(range(len(self.near), self.chips))
        cut = -(-self.per_chip * 3 // 5)
        self.pieces = [(0, cut)]
        if cut < self.per_chip:
            self.pieces.append((cut, self.per_chip - cut))

    def head(self, chip, slot):
        return chip * self.per_chip + slot


def pack_kernel(plan, items, me_ref, x_ref, ids_ref, counts_ref, *refs):
    outs, (wide, ids, counts, info, sem) = refs[: len(items)], refs[len(items) :]
    rows, _, heads, _ = x_ref.shape
    chip, lists = me_ref[0] // 2, plan.lists
    first = pl.program_id(0) == 0
    copies = [
        pltpu.make_async_copy(ids_ref, ids, sem.at[0]),
        pltpu.make_async_copy(counts_ref, counts, sem.at[1]),
    ]

    @pl.when(first)
    def _():
        for copy in copies:
            copy.start()

    def widen(t, carry):
        wide[pl.ds(pl.multiple_of(t * heads, 8), heads), :] = x_ref[t, 0].astype(F32)
        return carry

    lax.fori_loop(0, rows, widen, 0, unroll=8)

    @pl.when(first)
    def _():
        for copy in copies:
            copy.wait()
        info[...] = jnp.zeros_like(info)
        info[:lists, :heads] = ids[0].astype(F32)
        info[lists : lists + 1, :heads] = counts[...].astype(F32)

    for (step, start, size), out in zip(items, outs):
        for slot in range(size):
            head = jnp.minimum(plan.head(chip ^ step, start + slot), heads - 1)
            out[0, slot * rows : (slot + 1) * rows, :] = wide[
                pl.ds(head, rows, stride=heads), :
            ].astype(BF16)
        out[0, size * rows :, :] = info[...].astype(BF16)


def pack(plan, items, me, by_kind, block_ids, counts):
    rows, kinds, heads, dim = by_kind.shape
    depths = [size * rows + INFO_ROWS for _, _, size in items]
    block_ids = jnp.transpose(block_ids, (0, 2, 1))
    return pl.pallas_call(
        functools.partial(pack_kernel, plan, items),
        grid_spec=pltpu.PrefetchScalarGridSpec(
            num_scalar_prefetch=1,
            grid=(kinds,),
            in_specs=[
                pl.BlockSpec((rows, 1, heads, dim), lambda s, *_: (0, s, 0, 0)),
                pl.BlockSpec(memory_space=pl.ANY),
                pl.BlockSpec(memory_space=pl.ANY),
            ],
            out_specs=[pl.BlockSpec((1, d, dim), lambda s, *_: (s, 0, 0)) for d in depths],
            scratch_shapes=[
                pltpu.VMEM((rows * heads, dim), F32),
                pltpu.VMEM(block_ids.shape, I32),
                pltpu.VMEM(counts.shape, I32),
                pltpu.VMEM((INFO_ROWS, dim), F32),
                pltpu.SemaphoreType.DMA((2,)),
            ],
        ),
        out_shape=[jax.ShapeDtypeStruct((kinds, d, dim), BF16) for d in depths],
        compiler_params=params(PACK_BYTES),
        cost_estimate=cost(0, 8 << 20),
        name="pack",
    )(me, by_kind, block_ids, counts)


def gather_kernel(plan, spans, *refs):
    rows_refs, out_ref, sem = refs[:-2], refs[-2], refs[-1]
    copies = [
        pltpu.make_async_copy(ref.at[1:3, begin:end], out_ref.at[step], sem.at[step])
        for step, (ref, (begin, end)) in enumerate(zip(rows_refs, spans))
    ]
    for copy in copies:
        copy.start()
    for copy in copies:
        copy.wait()


def spans_of(plan, piece):
    first, size = piece
    begins = [(first if step in plan.near else 0) * plan.rows for step in range(plan.chips)]
    return [(begin, begin + size * plan.rows) for begin in begins]


def gather_keys(plan, piece, came):
    return pl.pallas_call(
        functools.partial(gather_kernel, plan, spans_of(plan, piece)),
        in_specs=[pl.BlockSpec(memory_space=pl.ANY)] * plan.chips,
        out_specs=pl.BlockSpec(memory_space=pl.ANY),
        out_shape=jax.ShapeDtypeStruct((plan.chips, 2, piece[1] * plan.rows, plan.dim), BF16),
        scratch_shapes=[pltpu.SemaphoreType.DMA((plan.chips,))],
        compiler_params=params(),
        cost_estimate=cost(0, 4 << 20),
        name="gather_keys",
    )(*came)


def attend_group(units, scale):
    scores = [
        lax.dot_general(q, k, (((1,), (1,)), ((), ())), preferred_element_type=F32)
        for q, k, _, _ in units
    ]
    scores = [s * scale + bias for s, (_, _, _, bias) in zip(scores, units)]
    peaks = [jnp.max(s, axis=1, keepdims=True) for s in scores]
    weights = [jnp.exp2(s - peak) for s, peak in zip(scores, peaks)]
    totals = [jnp.sum(w, axis=1, keepdims=True) for w in weights]
    mixed = [
        jnp.dot(w.astype(BF16), v, preferred_element_type=F32)
        for w, (_, _, v, _) in zip(weights, units)
    ]
    return [(m / t).astype(BF16) for m, t in zip(mixed, totals)]


def attend_kernel(plan, piece, scale, held_rows, me_ref, *refs):
    chips, rows, lists, bits = plan.chips, plan.rows, plan.lists, plan.bits
    first, size = piece
    near, far_ref, refs = refs[:chips], refs[chips], refs[chips + 1 :]
    helds = refs[: len(plan.near)] if held_rows else []
    refs = refs[len(helds) :]
    outs, refs = refs[:chips], refs[chips:]
    queries, keys, values, info, bias, code, scalars, sem = refs
    chip, core = me_ref[0] // 2, me_ref[0] % 2

    copies = []
    for step, (ref, (begin, end)) in enumerate(zip(near, spans_of(plan, piece))):
        last = ref.shape[1] - INFO_ROWS
        moves = [
            (ref.at[0, last:], info.at[step]),
            (ref.at[0, begin:end], queries.at[step]),
            (ref.at[1, begin:end], keys.at[2 * step]),
            (ref.at[2, begin:end], values.at[2 * step]),
            (far_ref.at[step, 0], keys.at[2 * step + 1]),
            (far_ref.at[step, 1], values.at[2 * step + 1]),
        ]
        copies += [
            pltpu.make_async_copy(source, target, sem.at[step, at])
            for at, (source, target) in enumerate(moves)
        ]
    for copy in copies:
        copy.start()

    count = lax.broadcasted_iota(I32, bias.shape, 0)
    entry = lax.broadcasted_iota(I32, bias.shape, 1) // rows
    bias[...] = jnp.where((entry < count) | (entry == 0), 0.0, DEAD).astype(F32)
    for held, out in zip(helds, outs):
        out[:held_rows, :] = held[...]
    for copy in copies:
        copy.wait()

    for step in range(chips):
        row = info[step].astype(F32).astype(I32)
        total = row[:1]
        for j in range(1, lists + 1):
            total = total + (row[j : j + 1] << (j * bits))
        code[step : step + 1, :] = total
    copy = pltpu.make_async_copy(code, scalars, sem.at[0, 0])
    copy.start()
    copy.wait()

    mask = (1 << bits) - 1

    def place(block):
        return ((block // 2) ^ chip) * 2 + ((block % 2) ^ core)

    def one_slot(slot, carry):
        head = jnp.minimum(plan.head(chip, first + slot), plan.heads - 1)
        span = pl.ds(pl.multiple_of(slot * rows, rows), rows)
        below = pl.ds(pl.multiple_of(held_rows + slot * rows, rows), rows)
        for start in range(0, chips, GROUP):
            steps, units = range(start, min(start + GROUP, chips)), []
            for step in steps:
                number = scalars[step, head]
                places = [place((number >> (j * bits)) & mask) for j in range(lists)]
                live = number >> (lists * bits)
                units.append(
                    (
                        queries[step, span, :],
                        jnp.concatenate([keys[c, span, :] for c in places], axis=0),
                        jnp.concatenate([values[c, span, :] for c in places], axis=0),
                        bias[pl.ds(live, 1), :],
                    )
                )
            for step, result in zip(steps, attend_group(units, scale)):
                outs[step][below if step in plan.near else span, :] = result
        return carry

    lax.fori_loop(0, size, one_slot, 0)


def attend(plan, piece, me, came, far, helds, scale):
    chips, dim, depth = plan.chips, plan.dim, piece[1] * plan.rows
    held_rows = helds[0].shape[0] if helds else 0
    bias_rows = -(-(plan.lists + 1) // 8) * 8
    any_spec = pl.BlockSpec(memory_space=pl.ANY)
    vmem_spec = pl.BlockSpec(memory_space=pltpu.VMEM)
    depths = [depth + (held_rows if step in plan.near else 0) for step in range(chips)]
    return pl.pallas_call(
        functools.partial(attend_kernel, plan, piece, scale, held_rows),
        in_specs=[pl.BlockSpec(memory_space=pltpu.SMEM)]
        + [any_spec] * (chips + 1)
        + [vmem_spec] * len(helds),
        out_specs=[vmem_spec] * chips,
        out_shape=[jax.ShapeDtypeStruct((d, dim), BF16) for d in depths],
        scratch_shapes=[
            pltpu.VMEM((chips, depth, dim), BF16),
            pltpu.VMEM((2 * chips, depth, dim), BF16),
            pltpu.VMEM((2 * chips, depth, dim), BF16),
            pltpu.VMEM((chips, INFO_ROWS, dim), BF16),
            pltpu.VMEM((bias_rows, plan.lists * plan.rows), F32),
            pltpu.VMEM((chips, dim), I32),
            pltpu.SMEM((chips, dim), I32),
            pltpu.SemaphoreType.DMA((chips, 6)),
        ],
        compiler_params=params(),
        cost_estimate=cost(4 << 30, 8 << 20),
        name="attend",
    )(me, *came, far, *helds)


def unpack_kernel(plan, items, me_ref, *refs):
    backs, (out_ref, wide) = refs[:-2], refs[-2:]
    rows, heads, _ = out_ref.shape
    chip = me_ref[0] // 2
    for (step, first, size), back in zip(items, backs):
        for slot in range(size):
            head = plan.head(chip ^ step, first + slot)

            def spread(back=back, head=head, slot=slot):
                wide[pl.ds(head, rows, stride=heads), :] = back[
                    slot * rows : (slot + 1) * rows, :
                ].astype(F32)

            if plan.padded:
                pl.when(head < heads)(spread)
            else:
                spread()

    def narrow(t, carry):
        out_ref[t] = wide[pl.ds(pl.multiple_of(t * heads, 8), heads), :].astype(BF16)
        return carry

    lax.fori_loop(0, rows, narrow, 0, unroll=8)


def unpack(plan, items, me, backs):
    rows, heads, dim = plan.rows, plan.heads, plan.dim
    vmem_spec = pl.BlockSpec(memory_space=pltpu.VMEM)
    return pl.pallas_call(
        functools.partial(unpack_kernel, plan, items),
        in_specs=[pl.BlockSpec(memory_space=pltpu.SMEM)] + [vmem_spec] * len(backs),
        out_specs=vmem_spec,
        out_shape=jax.ShapeDtypeStruct((rows, heads, dim), BF16),
        scratch_shapes=[pltpu.VMEM((rows * heads, dim), F32)],
        compiler_params=params(),
        cost_estimate=cost(0, 4 << 20),
        name="unpack",
    )(me, *backs)


class Sender:
    def __init__(self, seq):
        self.seq, self.ended = seq, []

    def send(self, array, step, after=None):
        if after is not None:
            array, _ = lax.optimization_barrier((array, after))
        if len(self.ended) >= WINDOW:
            array, _ = lax.optimization_barrier((array, self.ended[-WINDOW]))
        got = lax.ppermute(array, "seq", [(d, d ^ (2 * step)) for d in range(self.seq)])
        self.ended.append(got)
        return got


def mixed(far, near):
    order, far, near = far[:2], far[2:], near[1:]
    while far or near:
        order += near[:1] + far[:1]
        near, far = near[1:], far[1:]
    return order


def body(seq, qkv, block_ids, counts):
    rows, heads, _, dim = qkv.shape
    plan = Plan(seq, heads, rows, dim, block_ids.shape[2], seq * block_ids.shape[0])
    scale = math.log2(math.e) / math.sqrt(dim)
    me = lax.axis_index("seq").astype(I32).reshape(1)
    by_kind = jnp.transpose(qkv, (0, 2, 1, 3))
    near, far, pieces = plan.near, plan.far, plan.pieces
    sender = Sender(seq)

    def work(piece, came, helds, sent):
        if sent is not None:
            came, _ = lax.optimization_barrier((came, sent))
        swapped = gather_keys(plan, piece, came)
        swapped = lax.ppermute(swapped, "seq", [(d, d ^ 1) for d in range(seq)])
        return attend(plan, piece, me, came, swapped, helds, scale)

    far_items = [[(step, *piece) for step in far] for piece in pieces]
    near_items = [(step, 0, plan.per_chip) for step in near]
    rest_items = near_items + [item for items in far_items[1:] for item in items]
    packed = pack(plan, far_items[0], me, by_kind, block_ids, counts)
    rest = pack(plan, rest_items, me, by_kind, block_ids, counts)
    leaving = dict(zip(near, rest)) | dict(zip(far, packed))
    got = {step: sender.send(leaving[step], step) for step in mixed(far, near)}
    got[0] = rest[0]
    came = [got[step] for step in range(plan.chips)]
    backs = []
    if len(pieces) == 1:
        outs = work(pieces[0], came, [], None)
    else:
        last = rest[len(near) :]
        got = [sender.send(a, step) for a, step in zip(last[:LATE_A], far)]
        held = work(pieces[0], came, [], got[SEEN_A])
        got += [sender.send(a, step, held[0]) for a, step in zip(last[LATE_A:], far[LATE_A:])]
        came = came[: len(near)] + got
        leaving = held[len(near) :]
        got = [sender.send(a, step) for a, step in zip(leaving[:LATE_B], far)]
        outs = work(pieces[1], came, held[: len(near)], got[SEEN_B])
        got += [sender.send(a, step, outs[0]) for a, step in zip(leaving[LATE_B:], far[LATE_B:])]
        backs += got
    got = {step: sender.send(outs[step], step) for step in (mixed(far, near) if MIX_BACK else far + near[1:])}
    got[0] = outs[0]
    items = near_items + (far_items[0] if len(pieces) > 1 else []) + far_items[-1]
    backs = [got[step] for step in near] + backs + [got[step] for step in far]
    return unpack(plan, items, me, backs)


def solution(mesh):
    in_specs = (
        P(("rep", "seq"), None, None, None),
        P(("rep", "seq"), None, None),
        P(("rep", "seq"), None),
    )
    out_specs = P(("rep", "seq"), None, None)
    return jax.shard_map(
        functools.partial(body, mesh.shape["seq"]),
        mesh=mesh,
        in_specs=in_specs,
        out_specs=out_specs,
        check_vma=False,
    )
```

```python
import functools
import math

import jax
import jax.numpy as jnp
from jax import lax
from jax.experimental import pallas as pl
from jax.experimental.pallas import tpu as pltpu
from jax.sharding import PartitionSpec as P

F32, BF16, I32 = jnp.float32, jnp.bfloat16, jnp.int32
DEAD = -1e30
VMEM_BYTES = 48 << 20
INFO_ROWS = 16
GROUP = 4
CUT = 3
WINDOW = 8
LATE_A = 3
SEEN_A = 0
LATE_B = 5
SEEN_B = 1
WINDOW_LAST = 99


def params():
    return pltpu.CompilerParams(vmem_limit_bytes=VMEM_BYTES)


def cost(flops, count):
    return pl.CostEstimate(flops=flops, bytes_accessed=count, transcendentals=0)


class Plan:
    def __init__(self, seq, heads, rows, dim, lists, blocks):
        self.seq, self.heads, self.rows, self.dim, self.lists = seq, heads, rows, dim, lists
        self.chips = seq // 2
        self.per_chip = -(-heads // self.chips)
        self.padded = self.per_chip * self.chips > heads
        self.bits = max(1, (blocks - 1).bit_length())
        assert self.chips & (self.chips - 1) == 0
        assert lists * self.bits + lists.bit_length() < 31 and lists < INFO_ROWS
        self.near = list(range(max(1, self.chips // 2)))
        self.far = list(range(len(self.near), self.chips))
        cut = -(-self.per_chip * CUT // 5)
        self.pieces = [(0, cut)]
        if cut < self.per_chip:
            self.pieces.append((cut, self.per_chip - cut))

    def head(self, chip, slot):
        return chip * self.per_chip + slot


def pack_kernel(plan, items, me_ref, x_ref, ids_ref, counts_ref, *refs):
    outs, (wide, ids, counts, info, sem) = refs[: len(items)], refs[len(items) :]
    rows, _, heads, _ = x_ref.shape
    chip, lists = me_ref[0] // 2, plan.lists
    first = pl.program_id(0) == 0
    copies = [
        pltpu.make_async_copy(ids_ref, ids, sem.at[0]),
        pltpu.make_async_copy(counts_ref, counts, sem.at[1]),
    ]

    @pl.when(first)
    def _():
        for copy in copies:
            copy.start()

    def widen(t, carry):
        wide[pl.ds(pl.multiple_of(t * heads, 8), heads), :] = x_ref[t, 0].astype(F32)
        return carry

    lax.fori_loop(0, rows, widen, 0, unroll=8)

    @pl.when(first)
    def _():
        for copy in copies:
            copy.wait()
        info[...] = jnp.zeros_like(info)
        info[:lists, :heads] = ids[0].astype(F32)
        info[lists : lists + 1, :heads] = counts[...].astype(F32)

    for (step, start, size), out in zip(items, outs):
        for slot in range(size):
            head = jnp.minimum(plan.head(chip ^ step, start + slot), heads - 1)
            out[0, slot * rows : (slot + 1) * rows, :] = wide[
                pl.ds(head, rows, stride=heads), :
            ].astype(BF16)
        out[0, size * rows :, :] = info[...].astype(BF16)


def pack(plan, items, me, by_kind, block_ids, counts):
    rows, kinds, heads, dim = by_kind.shape
    depths = [size * rows + INFO_ROWS for _, _, size in items]
    block_ids = jnp.transpose(block_ids, (0, 2, 1))
    return pl.pallas_call(
        functools.partial(pack_kernel, plan, items),
        grid_spec=pltpu.PrefetchScalarGridSpec(
            num_scalar_prefetch=1,
            grid=(kinds,),
            in_specs=[
                pl.BlockSpec((rows, 1, heads, dim), lambda s, *_: (0, s, 0, 0)),
                pl.BlockSpec(memory_space=pl.ANY),
                pl.BlockSpec(memory_space=pl.ANY),
            ],
            out_specs=[pl.BlockSpec((1, d, dim), lambda s, *_: (s, 0, 0)) for d in depths],
            scratch_shapes=[
                pltpu.VMEM((rows * heads, dim), F32),
                pltpu.VMEM(block_ids.shape, I32),
                pltpu.VMEM(counts.shape, I32),
                pltpu.VMEM((INFO_ROWS, dim), F32),
                pltpu.SemaphoreType.DMA((2,)),
            ],
        ),
        out_shape=[jax.ShapeDtypeStruct((kinds, d, dim), BF16) for d in depths],
        compiler_params=params(),
        cost_estimate=cost(0, 8 << 20),
        name="pack",
    )(me, by_kind, block_ids, counts)


def gather_kernel(plan, spans, *refs):
    rows_refs, out_ref, sem = refs[:-2], refs[-2], refs[-1]
    copies = [
        pltpu.make_async_copy(ref.at[1:3, begin:end], out_ref.at[step], sem.at[step])
        for step, (ref, (begin, end)) in enumerate(zip(rows_refs, spans))
    ]
    for copy in copies:
        copy.start()
    for copy in copies:
        copy.wait()


def spans_of(plan, piece):
    first, size = piece
    begins = [(first if step in plan.near else 0) * plan.rows for step in range(plan.chips)]
    return [(begin, begin + size * plan.rows) for begin in begins]


def gather_keys(plan, piece, came):
    return pl.pallas_call(
        functools.partial(gather_kernel, plan, spans_of(plan, piece)),
        in_specs=[pl.BlockSpec(memory_space=pl.ANY)] * plan.chips,
        out_specs=pl.BlockSpec(memory_space=pl.ANY),
        out_shape=jax.ShapeDtypeStruct((plan.chips, 2, piece[1] * plan.rows, plan.dim), BF16),
        scratch_shapes=[pltpu.SemaphoreType.DMA((plan.chips,))],
        compiler_params=params(),
        cost_estimate=cost(0, 4 << 20),
        name="gather_keys",
    )(*came)


def attend_group(units, scale):
    scores = [
        lax.dot_general(q, k, (((1,), (1,)), ((), ())), preferred_element_type=F32)
        for q, k, _, _ in units
    ]
    scores = [s * scale + bias for s, (_, _, _, bias) in zip(scores, units)]
    peaks = [jnp.max(s, axis=1, keepdims=True) for s in scores]
    weights = [jnp.exp2(s - peak) for s, peak in zip(scores, peaks)]
    totals = [jnp.sum(w, axis=1, keepdims=True) for w in weights]
    mixed = [
        jnp.dot(w.astype(BF16), v, preferred_element_type=F32)
        for w, (_, _, v, _) in zip(weights, units)
    ]
    return [(m / t).astype(BF16) for m, t in zip(mixed, totals)]


def attend_kernel(plan, piece, scale, me_ref, *refs):
    chips, rows, lists, bits = plan.chips, plan.rows, plan.lists, plan.bits
    first, size = piece
    came, mine_ref, far_ref, refs = refs[:chips], refs[chips], refs[chips + 1], refs[chips + 2 :]
    outs, (queries, pairs, info, bias, code, scalars, sem, slot_sem) = refs[:chips], refs[chips:]
    chip, core = me_ref[0] // 2, me_ref[0] % 2

    info_copies, query_copies = [], []
    for step, (ref, (begin, end)) in enumerate(zip(came, spans_of(plan, piece))):
        last = ref.shape[1] - INFO_ROWS
        info_copies.append(
            pltpu.make_async_copy(ref.at[0, last:], info.at[step], sem.at[0, step])
        )
        query_copies.append(
            pltpu.make_async_copy(ref.at[0, begin:end], queries.at[step], sem.at[1, step])
        )

    def span_of(slot):
        return pl.ds(pl.multiple_of(slot * rows, rows), rows)

    def pair_copies(slot):
        span = span_of(slot)
        return [
            pltpu.make_async_copy(
                ref.at[:, :, span], pairs.at[at, :, :, span], slot_sem.at[at, slot]
            )
            for at, ref in enumerate((mine_ref, far_ref))
        ]

    for copy in info_copies + query_copies:
        copy.start()
    for slot in range(size):
        for copy in pair_copies(slot):
            copy.start()

    count = lax.broadcasted_iota(I32, bias.shape, 0)
    entry = lax.broadcasted_iota(I32, bias.shape, 1) // rows
    bias[...] = jnp.where((entry < count) | (entry == 0), 0.0, DEAD).astype(F32)
    for copy in info_copies:
        copy.wait()

    for step in range(chips):
        row = info[step].astype(F32).astype(I32)
        total = row[:1]
        for j in range(1, lists + 1):
            total = total + (row[j : j + 1] << (j * bits))
        code[step : step + 1, :] = total
    copy = pltpu.make_async_copy(code, scalars, sem.at[0, 0])
    copy.start()
    copy.wait()
    for copy in query_copies:
        copy.wait()

    mask = (1 << bits) - 1

    def one_slot(slot, carry):
        head = jnp.minimum(plan.head(chip, first + slot), plan.heads - 1)
        span = span_of(slot)
        for copy in pair_copies(slot):
            copy.wait()

        def pick(block, kind):
            return pairs[(block % 2) ^ core, (block // 2) ^ chip, kind, span, :]

        for start in range(0, chips, GROUP):
            steps, units = range(start, min(start + GROUP, chips)), []
            for step in steps:
                number = scalars[step, head]
                blocks = [(number >> (j * bits)) & mask for j in range(lists)]
                live = number >> (lists * bits)
                units.append(
                    (
                        queries[step, span, :],
                        jnp.concatenate([pick(block, 0) for block in blocks], axis=0),
                        jnp.concatenate([pick(block, 1) for block in blocks], axis=0),
                        bias[pl.ds(live, 1), :],
                    )
                )
            for step, result in zip(steps, attend_group(units, scale)):
                outs[step][span, :] = result
        return carry

    lax.fori_loop(0, size, one_slot, 0)


def attend(plan, piece, me, came, mine, far, scale):
    chips, dim, depth = plan.chips, plan.dim, piece[1] * plan.rows
    bias_rows = -(-(plan.lists + 1) // 8) * 8
    return pl.pallas_call(
        functools.partial(attend_kernel, plan, piece, scale),
        in_specs=[pl.BlockSpec(memory_space=pltpu.SMEM)]
        + [pl.BlockSpec(memory_space=pl.ANY)] * (chips + 2),
        out_specs=[pl.BlockSpec(memory_space=pltpu.VMEM)] * chips,
        out_shape=[jax.ShapeDtypeStruct((depth, dim), BF16)] * chips,
        scratch_shapes=[
            pltpu.VMEM((chips, depth, dim), BF16),
            pltpu.VMEM((2, chips, 2, depth, dim), BF16),
            pltpu.VMEM((chips, INFO_ROWS, dim), BF16),
            pltpu.VMEM((bias_rows, plan.lists * plan.rows), F32),
            pltpu.VMEM((chips, dim), I32),
            pltpu.SMEM((chips, dim), I32),
            pltpu.SemaphoreType.DMA((2, chips)),
            pltpu.SemaphoreType.DMA((2, piece[1])),
        ],
        compiler_params=params(),
        cost_estimate=cost(4 << 30, 8 << 20),
        name="attend",
    )(me, *came, mine, far)


def unpack_kernel(plan, items, me_ref, *refs):
    backs, (out_ref, wide) = refs[:-2], refs[-2:]
    rows, heads, _ = out_ref.shape
    chip = me_ref[0] // 2
    for (step, first, size), back in zip(items, backs):
        for slot in range(size):
            head = plan.head(chip ^ step, first + slot)

            def spread(back=back, head=head, slot=slot):
                wide[pl.ds(head, rows, stride=heads), :] = back[
                    slot * rows : (slot + 1) * rows, :
                ].astype(F32)

            if plan.padded:
                pl.when(head < heads)(spread)
            else:
                spread()

    def narrow(t, carry):
        out_ref[t] = wide[pl.ds(pl.multiple_of(t * heads, 8), heads), :].astype(BF16)
        return carry

    lax.fori_loop(0, rows, narrow, 0, unroll=8)


def unpack(plan, items, me, backs):
    rows, heads, dim = plan.rows, plan.heads, plan.dim
    vmem_spec = pl.BlockSpec(memory_space=pltpu.VMEM)
    return pl.pallas_call(
        functools.partial(unpack_kernel, plan, items),
        in_specs=[pl.BlockSpec(memory_space=pltpu.SMEM)] + [vmem_spec] * len(backs),
        out_specs=vmem_spec,
        out_shape=jax.ShapeDtypeStruct((rows, heads, dim), BF16),
        scratch_shapes=[pltpu.VMEM((rows * heads, dim), F32)],
        compiler_params=params(),
        cost_estimate=cost(0, 4 << 20),
        name="unpack",
    )(me, *backs)


class Sender:
    def __init__(self, seq):
        self.seq, self.ended = seq, []

    def send(self, array, step, after=None, window=WINDOW):
        if after is not None:
            array, _ = lax.optimization_barrier((array, after))
        if len(self.ended) >= window:
            array, _ = lax.optimization_barrier((array, self.ended[-window]))
        got = lax.ppermute(array, "seq", [(d, d ^ (2 * step)) for d in range(self.seq)])
        self.ended.append(got)
        return got


def mixed(far, near):
    order, far, near = far[:2], far[2:], near[1:]
    while far or near:
        order += near[:1] + far[:1]
        near, far = near[1:], far[1:]
    return order


def body(seq, qkv, block_ids, counts):
    rows, heads, _, dim = qkv.shape
    plan = Plan(seq, heads, rows, dim, block_ids.shape[2], seq * block_ids.shape[0])
    scale = math.log2(math.e) / math.sqrt(dim)
    me = lax.axis_index("seq").astype(I32).reshape(1)
    by_kind = jnp.transpose(qkv, (0, 2, 1, 3))
    near, far, pieces = plan.near, plan.far, plan.pieces
    sender = Sender(seq)

    def work(piece, came, sent):
        if sent is not None:
            came, _ = lax.optimization_barrier((came, sent))
        mine = gather_keys(plan, piece, came)
        swapped = lax.ppermute(mine, "seq", [(d, d ^ 1) for d in range(seq)])
        return attend(plan, piece, me, came, mine, swapped, scale)

    far_items = [[(step, *piece) for step in far] for piece in pieces]
    near_items = [(step, 0, plan.per_chip) for step in near]
    rest_items = near_items + [item for items in far_items[1:] for item in items]
    packed = pack(plan, far_items[0], me, by_kind, block_ids, counts)
    rest = pack(plan, rest_items, me, by_kind, block_ids, counts)
    leaving = dict(zip(near, rest)) | dict(zip(far, packed))
    got = {step: sender.send(leaving[step], step) for step in mixed(far, near)}
    got[0] = rest[0]
    came = [got[step] for step in range(plan.chips)]
    items, backs = [], []

    def keep(piece, got):
        items.extend((step, *piece) for step in range(plan.chips))
        backs.extend(got[step] for step in range(plan.chips))

    if len(pieces) == 1:
        outs = work(pieces[0], came, None)
    else:
        last = rest[len(near) :]
        got = [sender.send(a, step) for a, step in zip(last[:LATE_A], far)]
        held = work(pieces[0], came, got[SEEN_A])
        got += [sender.send(a, step, held[0]) for a, step in zip(last[LATE_A:], far[LATE_A:])]
        came = came[: len(near)] + got
        got, order = {0: held[0]}, mixed(far, near)
        for step in order[:LATE_B]:
            got[step] = sender.send(held[step], step)
        outs = work(pieces[1], came, got[order[SEEN_B]])
        for step in order[LATE_B:]:
            got[step] = sender.send(held[step], step, outs[0])
        keep(pieces[0], got)
    got = {0: outs[0]}
    for step in mixed(far, near):
        got[step] = sender.send(outs[step], step, window=WINDOW_LAST)
    keep(pieces[-1], got)
    return unpack(plan, items, me, backs)


def solution(mesh):
    in_specs = (
        P(("rep", "seq"), None, None, None),
        P(("rep", "seq"), None, None),
        P(("rep", "seq"), None),
    )
    out_specs = P(("rep", "seq"), None, None)
    return jax.shard_map(
        functools.partial(body, mesh.shape["seq"]),
        mesh=mesh,
        in_specs=in_specs,
        out_specs=out_specs,
        check_vma=False,
    )
```

```python
import functools
import math

import jax
import jax.numpy as jnp
from jax import lax
from jax.experimental import pallas as pl
from jax.experimental.pallas import tpu as pltpu
from jax.sharding import PartitionSpec as P

F32, BF16, I32 = jnp.float32, jnp.bfloat16, jnp.int32
DEAD = -1e30
VMEM_BYTES = 48 << 20
INFO_ROWS = 16
GROUP = 4
CUT = 3
WINDOW = 8
LATE_A = 3
SEEN_A = 0
LATE_B = 5
SEEN_B = 1
WINDOW_LAST = 99


def params():
    return pltpu.CompilerParams(vmem_limit_bytes=VMEM_BYTES)


def cost(flops, count):
    return pl.CostEstimate(flops=flops, bytes_accessed=count, transcendentals=0)


class Plan:
    def __init__(self, seq, heads, rows, dim, lists, blocks):
        self.seq, self.heads, self.rows, self.dim, self.lists = seq, heads, rows, dim, lists
        self.chips = seq // 2
        self.per_chip = -(-heads // self.chips)
        self.padded = self.per_chip * self.chips > heads
        self.bits = max(1, (blocks - 1).bit_length())
        assert self.chips & (self.chips - 1) == 0
        assert lists * self.bits + lists.bit_length() < 31 and lists < INFO_ROWS
        self.near = list(range(max(1, self.chips // 2)))
        self.far = list(range(len(self.near), self.chips))
        cut = -(-self.per_chip * CUT // 5)
        self.pieces = [(0, cut)]
        if cut < self.per_chip:
            self.pieces.append((cut, self.per_chip - cut))

    def head(self, chip, slot):
        return chip * self.per_chip + slot


def pack_kernel(plan, items, me_ref, x_ref, ids_ref, counts_ref, *refs):
    outs, (wide, ids, counts, info, sem) = refs[: len(items)], refs[len(items) :]
    rows, _, heads, _ = x_ref.shape
    chip, lists = me_ref[0] // 2, plan.lists
    first = pl.program_id(0) == 0
    copies = [
        pltpu.make_async_copy(ids_ref, ids, sem.at[0]),
        pltpu.make_async_copy(counts_ref, counts, sem.at[1]),
    ]

    @pl.when(first)
    def _():
        for copy in copies:
            copy.start()

    def widen(t, carry):
        wide[pl.ds(pl.multiple_of(t * heads, 8), heads), :] = x_ref[t, 0].astype(F32)
        return carry

    lax.fori_loop(0, rows, widen, 0, unroll=8)

    @pl.when(first)
    def _():
        for copy in copies:
            copy.wait()
        info[...] = jnp.zeros_like(info)
        info[:lists, :heads] = ids[0].astype(F32)
        info[lists : lists + 1, :heads] = counts[...].astype(F32)

    for (step, start, size), out in zip(items, outs):
        for slot in range(size):
            head = jnp.minimum(plan.head(chip ^ step, start + slot), heads - 1)
            out[0, slot * rows : (slot + 1) * rows, :] = wide[
                pl.ds(head, rows, stride=heads), :
            ].astype(BF16)
        out[0, size * rows :, :] = info[...].astype(BF16)


def pack(plan, items, me, by_kind, block_ids, counts):
    rows, kinds, heads, dim = by_kind.shape
    depths = [size * rows + INFO_ROWS for _, _, size in items]
    block_ids = jnp.transpose(block_ids, (0, 2, 1))
    return pl.pallas_call(
        functools.partial(pack_kernel, plan, items),
        grid_spec=pltpu.PrefetchScalarGridSpec(
            num_scalar_prefetch=1,
            grid=(kinds,),
            in_specs=[
                pl.BlockSpec((rows, 1, heads, dim), lambda s, *_: (0, s, 0, 0)),
                pl.BlockSpec(memory_space=pl.ANY),
                pl.BlockSpec(memory_space=pl.ANY),
            ],
            out_specs=[pl.BlockSpec((1, d, dim), lambda s, *_: (s, 0, 0)) for d in depths],
            scratch_shapes=[
                pltpu.VMEM((rows * heads, dim), F32),
                pltpu.VMEM(block_ids.shape, I32),
                pltpu.VMEM(counts.shape, I32),
                pltpu.VMEM((INFO_ROWS, dim), F32),
                pltpu.SemaphoreType.DMA((2,)),
            ],
        ),
        out_shape=[jax.ShapeDtypeStruct((kinds, d, dim), BF16) for d in depths],
        compiler_params=params(),
        cost_estimate=cost(0, 8 << 20),
        name="pack",
    )(me, by_kind, block_ids, counts)


def gather_kernel(plan, spans, *refs):
    rows_refs, out_ref, sem = refs[:-2], refs[-2], refs[-1]
    copies = [
        pltpu.make_async_copy(ref.at[1:3, begin:end], out_ref.at[step], sem.at[step])
        for step, (ref, (begin, end)) in enumerate(zip(rows_refs, spans))
    ]
    for copy in copies:
        copy.start()
    for copy in copies:
        copy.wait()


def spans_of(plan, piece):
    first, size = piece
    begins = [(first if step in plan.near else 0) * plan.rows for step in range(plan.chips)]
    return [(begin, begin + size * plan.rows) for begin in begins]


def gather_keys(plan, piece, came):
    return pl.pallas_call(
        functools.partial(gather_kernel, plan, spans_of(plan, piece)),
        in_specs=[pl.BlockSpec(memory_space=pl.ANY)] * plan.chips,
        out_specs=pl.BlockSpec(memory_space=pl.ANY),
        out_shape=jax.ShapeDtypeStruct((plan.chips, 2, piece[1] * plan.rows, plan.dim), BF16),
        scratch_shapes=[pltpu.SemaphoreType.DMA((plan.chips,))],
        compiler_params=params(),
        cost_estimate=cost(0, 4 << 20),
        name="gather_keys",
    )(*came)


def attend_group(units, scale):
    scores = [
        lax.dot_general(q, k, (((1,), (1,)), ((), ())), preferred_element_type=F32)
        for q, k, _, _ in units
    ]
    scores = [s * scale + bias for s, (_, _, _, bias) in zip(scores, units)]
    peaks = [jnp.max(s, axis=1, keepdims=True) for s in scores]
    weights = [jnp.exp2(s - peak) for s, peak in zip(scores, peaks)]
    totals = [jnp.sum(w, axis=1, keepdims=True) for w in weights]
    mixed = [
        jnp.dot(w.astype(BF16), v, preferred_element_type=F32)
        for w, (_, _, v, _) in zip(weights, units)
    ]
    return [(m / t).astype(BF16) for m, t in zip(mixed, totals)]


def attend_kernel(plan, piece, scale, me_ref, *refs):
    chips, rows, lists, bits = plan.chips, plan.rows, plan.lists, plan.bits
    first, size = piece
    came, mine_ref, far_ref, refs = refs[:chips], refs[chips], refs[chips + 1], refs[chips + 2 :]
    outs, (queries, pairs, info, bias, code, scalars, sem, slot_sem) = refs[:chips], refs[chips:]
    chip, core = me_ref[0] // 2, me_ref[0] % 2

    info_copies, query_copies = [], []
    for step, (ref, (begin, end)) in enumerate(zip(came, spans_of(plan, piece))):
        last = ref.shape[1] - INFO_ROWS
        info_copies.append(
            pltpu.make_async_copy(ref.at[0, last:], info.at[step], sem.at[0, step])
        )
        query_copies.append(
            pltpu.make_async_copy(ref.at[0, begin:end], queries.at[step], sem.at[1, step])
        )

    def span_of(slot):
        return pl.ds(pl.multiple_of(slot * rows, rows), rows)

    def pair_copies(slot):
        span = span_of(slot)
        return [
            pltpu.make_async_copy(
                ref.at[:, :, span], pairs.at[at, :, :, span], slot_sem.at[at, slot]
            )
            for at, ref in enumerate((mine_ref, far_ref))
        ]

    for copy in info_copies + query_copies:
        copy.start()
    for slot in range(size):
        for copy in pair_copies(slot):
            copy.start()

    count = lax.broadcasted_iota(I32, bias.shape, 0)
    entry = lax.broadcasted_iota(I32, bias.shape, 1) // rows
    bias[...] = jnp.where((entry < count) | (entry == 0), 0.0, DEAD).astype(F32)
    for copy in info_copies:
        copy.wait()

    for step in range(chips):
        row = info[step].astype(F32).astype(I32)
        total = row[:1]
        for j in range(1, lists + 1):
            total = total + (row[j : j + 1] << (j * bits))
        code[step : step + 1, :] = total
    copy = pltpu.make_async_copy(code, scalars, sem.at[0, 0])
    copy.start()
    copy.wait()
    for copy in query_copies:
        copy.wait()

    mask = (1 << bits) - 1

    def one_slot(slot, carry):
        head = jnp.minimum(plan.head(chip, first + slot), plan.heads - 1)
        span = span_of(slot)
        for copy in pair_copies(slot):
            copy.wait()

        def pick(block, kind):
            return pairs[(block % 2) ^ core, (block // 2) ^ chip, kind, span, :]

        for start in range(0, chips, GROUP):
            steps, units = range(start, min(start + GROUP, chips)), []
            for step in steps:
                number = scalars[step, head]
                blocks = [(number >> (j * bits)) & mask for j in range(lists)]
                live = number >> (lists * bits)
                units.append(
                    (
                        queries[step, span, :],
                        jnp.concatenate([pick(block, 0) for block in blocks], axis=0),
                        jnp.concatenate([pick(block, 1) for block in blocks], axis=0),
                        bias[pl.ds(live, 1), :],
                    )
                )
            for step, result in zip(steps, attend_group(units, scale)):
                outs[step][span, :] = result
        return carry

    lax.fori_loop(0, size, one_slot, 0)


def attend(plan, piece, me, came, mine, far, scale):
    chips, dim, depth = plan.chips, plan.dim, piece[1] * plan.rows
    bias_rows = -(-(plan.lists + 1) // 8) * 8
    return pl.pallas_call(
        functools.partial(attend_kernel, plan, piece, scale),
        in_specs=[pl.BlockSpec(memory_space=pltpu.SMEM)]
        + [pl.BlockSpec(memory_space=pl.ANY)] * (chips + 2),
        out_specs=[pl.BlockSpec(memory_space=pltpu.VMEM)] * chips,
        out_shape=[jax.ShapeDtypeStruct((depth, dim), BF16)] * chips,
        scratch_shapes=[
            pltpu.VMEM((chips, depth, dim), BF16),
            pltpu.VMEM((2, chips, 2, depth, dim), BF16),
            pltpu.VMEM((chips, INFO_ROWS, dim), BF16),
            pltpu.VMEM((bias_rows, plan.lists * plan.rows), F32),
            pltpu.VMEM((chips, dim), I32),
            pltpu.SMEM((chips, dim), I32),
            pltpu.SemaphoreType.DMA((2, chips)),
            pltpu.SemaphoreType.DMA((2, piece[1])),
        ],
        compiler_params=params(),
        cost_estimate=cost(4 << 30, 8 << 20),
        name="attend",
    )(me, *came, mine, far)


def unpack_kernel(plan, items, me_ref, *refs):
    backs, (out_ref, wide) = refs[:-2], refs[-2:]
    rows, heads, _ = out_ref.shape
    chip = me_ref[0] // 2
    for (step, first, size), back in zip(items, backs):
        for slot in range(size):
            head = plan.head(chip ^ step, first + slot)

            def spread(back=back, head=head, slot=slot):
                wide[pl.ds(head, rows, stride=heads), :] = back[
                    slot * rows : (slot + 1) * rows, :
                ].astype(F32)

            if plan.padded:
                pl.when(head < heads)(spread)
            else:
                spread()

    def narrow(t, carry):
        out_ref[t] = wide[pl.ds(pl.multiple_of(t * heads, 8), heads), :].astype(BF16)
        return carry

    lax.fori_loop(0, rows, narrow, 0, unroll=8)


def unpack(plan, items, me, backs):
    rows, heads, dim = plan.rows, plan.heads, plan.dim
    vmem_spec = pl.BlockSpec(memory_space=pltpu.VMEM)
    return pl.pallas_call(
        functools.partial(unpack_kernel, plan, items),
        in_specs=[pl.BlockSpec(memory_space=pltpu.SMEM)] + [vmem_spec] * len(backs),
        out_specs=vmem_spec,
        out_shape=jax.ShapeDtypeStruct((rows, heads, dim), BF16),
        scratch_shapes=[pltpu.VMEM((rows * heads, dim), F32)],
        compiler_params=params(),
        cost_estimate=cost(0, 4 << 20),
        name="unpack",
    )(me, *backs)


class Sender:
    def __init__(self, seq):
        self.seq, self.ended = seq, []

    def send(self, array, step, after=None, window=WINDOW):
        if after is not None:
            array, _ = lax.optimization_barrier((array, after))
        if len(self.ended) >= window:
            array, _ = lax.optimization_barrier((array, self.ended[-window]))
        got = lax.ppermute(array, "seq", [(d, d ^ (2 * step)) for d in range(self.seq)])
        self.ended.append(got)
        return got


def mixed(far, near):
    far = far[::-1]
    order, far, near = far[:2], far[2:], near[1:]
    while far or near:
        order += near[:1] + far[:1]
        near, far = near[1:], far[1:]
    return order


def body(seq, qkv, block_ids, counts):
    rows, heads, _, dim = qkv.shape
    plan = Plan(seq, heads, rows, dim, block_ids.shape[2], seq * block_ids.shape[0])
    scale = math.log2(math.e) / math.sqrt(dim)
    me = lax.axis_index("seq").astype(I32).reshape(1)
    by_kind = jnp.transpose(qkv, (0, 2, 1, 3))
    near, far, pieces = plan.near, plan.far, plan.pieces
    sender = Sender(seq)

    def work(piece, came, sent):
        if sent is not None:
            came, _ = lax.optimization_barrier((came, sent))
        mine = gather_keys(plan, piece, came)
        swapped = lax.ppermute(mine, "seq", [(d, d ^ 1) for d in range(seq)])
        return attend(plan, piece, me, came, mine, swapped, scale)

    far_items = [[(step, *piece) for step in far] for piece in pieces]
    near_items = [(step, 0, plan.per_chip) for step in near]
    rest_items = near_items + [item for items in far_items[1:] for item in items]
    packed = pack(plan, far_items[0], me, by_kind, block_ids, counts)
    rest = pack(plan, rest_items, me, by_kind, block_ids, counts)
    leaving = dict(zip(near, rest)) | dict(zip(far, packed))
    got = {step: sender.send(leaving[step], step) for step in mixed(far, near)}
    got[0] = rest[0]
    came = [got[step] for step in range(plan.chips)]
    items, backs = [], []

    def keep(piece, got):
        items.extend((step, *piece) for step in range(plan.chips))
        backs.extend(got[step] for step in range(plan.chips))

    if len(pieces) == 1:
        outs = work(pieces[0], came, None)
    else:
        last = rest[len(near) :]
        got = [sender.send(a, step) for a, step in zip(last[:LATE_A], far)]
        held = work(pieces[0], came, got[SEEN_A])
        got += [sender.send(a, step, held[0]) for a, step in zip(last[LATE_A:], far[LATE_A:])]
        came = came[: len(near)] + got
        got, order = {0: held[0]}, mixed(far, near)
        for step in order[:LATE_B]:
            got[step] = sender.send(held[step], step)
        outs = work(pieces[1], came, got[order[SEEN_B]])
        for step in order[LATE_B:]:
            got[step] = sender.send(held[step], step, outs[0])
        keep(pieces[0], got)
    got = {0: outs[0]}
    for step in mixed(far, near):
        got[step] = sender.send(outs[step], step, window=WINDOW_LAST)
    keep(pieces[-1], got)
    return unpack(plan, items, me, backs)


def solution(mesh):
    in_specs = (
        P(("rep", "seq"), None, None, None),
        P(("rep", "seq"), None, None),
        P(("rep", "seq"), None),
    )
    out_specs = P(("rep", "seq"), None, None)
    return jax.shard_map(
        functools.partial(body, mesh.shape["seq"]),
        mesh=mesh,
        in_specs=in_specs,
        out_specs=out_specs,
        check_vma=False,
    )
```

```python
import functools
import math

import jax
import jax.numpy as jnp
from jax import lax
from jax.experimental import pallas as pl
from jax.experimental.pallas import tpu as pltpu
from jax.sharding import PartitionSpec as P

F32, BF16, I32 = jnp.float32, jnp.bfloat16, jnp.int32
DEAD = -1e30
VMEM_BYTES = 48 << 20
INFO_ROWS = 16
GROUP = 4
CUT = 3
WINDOW = 8
LATE_A = 4
SEEN_A = 0
LATE_B = 5
SEEN_B = 2
WINDOW_LAST = 99


def params():
    return pltpu.CompilerParams(vmem_limit_bytes=VMEM_BYTES)


def cost(flops, count):
    return pl.CostEstimate(flops=flops, bytes_accessed=count, transcendentals=0)


class Plan:
    def __init__(self, seq, heads, rows, dim, lists, blocks):
        self.seq, self.heads, self.rows, self.dim, self.lists = seq, heads, rows, dim, lists
        self.chips = seq // 2
        self.per_chip = -(-heads // self.chips)
        self.padded = self.per_chip * self.chips > heads
        self.bits = max(1, (blocks - 1).bit_length())
        assert self.chips & (self.chips - 1) == 0
        assert lists * self.bits + lists.bit_length() < 31 and lists < INFO_ROWS
        self.near = list(range(max(1, self.chips // 2)))
        self.far = list(range(len(self.near), self.chips))
        cut = -(-self.per_chip * CUT // 5)
        self.pieces = [(0, cut)]
        if cut < self.per_chip:
            self.pieces.append((cut, self.per_chip - cut))

    def head(self, chip, slot):
        return chip * self.per_chip + slot


def pack_kernel(plan, items, me_ref, x_ref, ids_ref, counts_ref, *refs):
    outs, (wide, ids, counts, info, sem) = refs[: len(items)], refs[len(items) :]
    rows, _, heads, _ = x_ref.shape
    chip, lists = me_ref[0] // 2, plan.lists
    first = pl.program_id(0) == 0
    copies = [
        pltpu.make_async_copy(ids_ref, ids, sem.at[0]),
        pltpu.make_async_copy(counts_ref, counts, sem.at[1]),
    ]

    @pl.when(first)
    def _():
        for copy in copies:
            copy.start()

    def widen(t, carry):
        wide[pl.ds(pl.multiple_of(t * heads, 8), heads), :] = x_ref[t, 0].astype(F32)
        return carry

    lax.fori_loop(0, rows, widen, 0, unroll=8)

    @pl.when(first)
    def _():
        for copy in copies:
            copy.wait()
        info[...] = jnp.zeros_like(info)
        info[:lists, :heads] = ids[0].astype(F32)
        info[lists : lists + 1, :heads] = counts[...].astype(F32)

    for (step, start, size), out in zip(items, outs):
        for slot in range(size):
            head = jnp.minimum(plan.head(chip ^ step, start + slot), heads - 1)
            out[0, slot * rows : (slot + 1) * rows, :] = wide[
                pl.ds(head, rows, stride=heads), :
            ].astype(BF16)
        out[0, size * rows :, :] = info[...].astype(BF16)


def pack(plan, items, me, by_kind, block_ids, counts):
    rows, kinds, heads, dim = by_kind.shape
    depths = [size * rows + INFO_ROWS for _, _, size in items]
    block_ids = jnp.transpose(block_ids, (0, 2, 1))
    return pl.pallas_call(
        functools.partial(pack_kernel, plan, items),
        grid_spec=pltpu.PrefetchScalarGridSpec(
            num_scalar_prefetch=1,
            grid=(kinds,),
            in_specs=[
                pl.BlockSpec((rows, 1, heads, dim), lambda s, *_: (0, s, 0, 0)),
                pl.BlockSpec(memory_space=pl.ANY),
                pl.BlockSpec(memory_space=pl.ANY),
            ],
            out_specs=[pl.BlockSpec((1, d, dim), lambda s, *_: (s, 0, 0)) for d in depths],
            scratch_shapes=[
                pltpu.VMEM((rows * heads, dim), F32),
                pltpu.VMEM(block_ids.shape, I32),
                pltpu.VMEM(counts.shape, I32),
                pltpu.VMEM((INFO_ROWS, dim), F32),
                pltpu.SemaphoreType.DMA((2,)),
            ],
        ),
        out_shape=[jax.ShapeDtypeStruct((kinds, d, dim), BF16) for d in depths],
        compiler_params=params(),
        cost_estimate=cost(0, 8 << 20),
        name="pack",
    )(me, by_kind, block_ids, counts)


def gather_kernel(plan, spans, *refs):
    rows_refs, out_ref, sem = refs[:-2], refs[-2], refs[-1]
    copies = [
        pltpu.make_async_copy(ref.at[1:3, begin:end], out_ref.at[step], sem.at[step])
        for step, (ref, (begin, end)) in enumerate(zip(rows_refs, spans))
    ]
    for copy in copies:
        copy.start()
    for copy in copies:
        copy.wait()


def spans_of(plan, piece):
    first, size = piece
    begins = [(first if step in plan.near else 0) * plan.rows for step in range(plan.chips)]
    return [(begin, begin + size * plan.rows) for begin in begins]


def gather_keys(plan, piece, came):
    return pl.pallas_call(
        functools.partial(gather_kernel, plan, spans_of(plan, piece)),
        in_specs=[pl.BlockSpec(memory_space=pl.ANY)] * plan.chips,
        out_specs=pl.BlockSpec(memory_space=pl.ANY),
        out_shape=jax.ShapeDtypeStruct((plan.chips, 2, piece[1] * plan.rows, plan.dim), BF16),
        scratch_shapes=[pltpu.SemaphoreType.DMA((plan.chips,))],
        compiler_params=params(),
        cost_estimate=cost(0, 4 << 20),
        name="gather_keys",
    )(*came)


def attend_group(units, scale):
    scores = [
        lax.dot_general(q, k, (((1,), (1,)), ((), ())), preferred_element_type=F32)
        for q, k, _, _ in units
    ]
    scores = [s * scale + bias for s, (_, _, _, bias) in zip(scores, units)]
    peaks = [jnp.max(s, axis=1, keepdims=True) for s in scores]
    weights = [jnp.exp2(s - peak) for s, peak in zip(scores, peaks)]
    totals = [jnp.sum(w, axis=1, keepdims=True) for w in weights]
    mixed = [
        jnp.dot(w.astype(BF16), v, preferred_element_type=F32)
        for w, (_, _, v, _) in zip(weights, units)
    ]
    return [(m / t).astype(BF16) for m, t in zip(mixed, totals)]


def attend_kernel(plan, piece, scale, me_ref, *refs):
    chips, rows, lists, bits = plan.chips, plan.rows, plan.lists, plan.bits
    first, size = piece
    came, mine_ref, far_ref, refs = refs[:chips], refs[chips], refs[chips + 1], refs[chips + 2 :]
    outs, (queries, pairs, info, bias, code, scalars, sem, slot_sem) = refs[:chips], refs[chips:]
    chip, core = me_ref[0] // 2, me_ref[0] % 2

    info_copies, query_copies = [], []
    for step, (ref, (begin, end)) in enumerate(zip(came, spans_of(plan, piece))):
        last = ref.shape[1] - INFO_ROWS
        info_copies.append(
            pltpu.make_async_copy(ref.at[0, last:], info.at[step], sem.at[0, step])
        )
        query_copies.append(
            pltpu.make_async_copy(ref.at[0, begin:end], queries.at[step], sem.at[1, step])
        )

    def span_of(slot):
        return pl.ds(pl.multiple_of(slot * rows, rows), rows)

    def pair_copies(slot):
        span = span_of(slot)
        return [
            pltpu.make_async_copy(
                ref.at[:, :, span], pairs.at[at, :, :, span], slot_sem.at[at, slot]
            )
            for at, ref in enumerate((mine_ref, far_ref))
        ]

    for copy in info_copies + query_copies:
        copy.start()
    for slot in range(size):
        for copy in pair_copies(slot):
            copy.start()

    count = lax.broadcasted_iota(I32, bias.shape, 0)
    entry = lax.broadcasted_iota(I32, bias.shape, 1) // rows
    bias[...] = jnp.where((entry < count) | (entry == 0), 0.0, DEAD).astype(F32)
    for copy in info_copies:
        copy.wait()

    for step in range(chips):
        row = info[step].astype(F32).astype(I32)
        total = row[:1]
        for j in range(1, lists + 1):
            total = total + (row[j : j + 1] << (j * bits))
        code[step : step + 1, :] = total
    copy = pltpu.make_async_copy(code, scalars, sem.at[0, 0])
    copy.start()
    copy.wait()
    for copy in query_copies:
        copy.wait()

    mask = (1 << bits) - 1

    def one_slot(slot, carry):
        head = jnp.minimum(plan.head(chip, first + slot), plan.heads - 1)
        span = span_of(slot)
        for copy in pair_copies(slot):
            copy.wait()

        def pick(block, kind):
            return pairs[(block % 2) ^ core, (block // 2) ^ chip, kind, span, :]

        for start in range(0, chips, GROUP):
            steps, units = range(start, min(start + GROUP, chips)), []
            for step in steps:
                number = scalars[step, head]
                blocks = [(number >> (j * bits)) & mask for j in range(lists)]
                live = number >> (lists * bits)
                units.append(
                    (
                        queries[step, span, :],
                        jnp.concatenate([pick(block, 0) for block in blocks], axis=0),
                        jnp.concatenate([pick(block, 1) for block in blocks], axis=0),
                        bias[pl.ds(live, 1), :],
                    )
                )
            for step, result in zip(steps, attend_group(units, scale)):
                outs[step][span, :] = result
        return carry

    lax.fori_loop(0, size, one_slot, 0)


def attend(plan, piece, me, came, mine, far, scale):
    chips, dim, depth = plan.chips, plan.dim, piece[1] * plan.rows
    bias_rows = -(-(plan.lists + 1) // 8) * 8
    return pl.pallas_call(
        functools.partial(attend_kernel, plan, piece, scale),
        in_specs=[pl.BlockSpec(memory_space=pltpu.SMEM)]
        + [pl.BlockSpec(memory_space=pl.ANY)] * (chips + 2),
        out_specs=[pl.BlockSpec(memory_space=pltpu.VMEM)] * chips,
        out_shape=[jax.ShapeDtypeStruct((depth, dim), BF16)] * chips,
        scratch_shapes=[
            pltpu.VMEM((chips, depth, dim), BF16),
            pltpu.VMEM((2, chips, 2, depth, dim), BF16),
            pltpu.VMEM((chips, INFO_ROWS, dim), BF16),
            pltpu.VMEM((bias_rows, plan.lists * plan.rows), F32),
            pltpu.VMEM((chips, dim), I32),
            pltpu.SMEM((chips, dim), I32),
            pltpu.SemaphoreType.DMA((2, chips)),
            pltpu.SemaphoreType.DMA((2, piece[1])),
        ],
        compiler_params=params(),
        cost_estimate=cost(4 << 30, 8 << 20),
        name="attend",
    )(me, *came, mine, far)


def unpack_kernel(plan, items, me_ref, *refs):
    backs, (out_ref, wide) = refs[:-2], refs[-2:]
    rows, heads, _ = out_ref.shape
    chip = me_ref[0] // 2
    for (step, first, size), back in zip(items, backs):
        for slot in range(size):
            head = plan.head(chip ^ step, first + slot)

            def spread(back=back, head=head, slot=slot):
                wide[pl.ds(head, rows, stride=heads), :] = back[
                    slot * rows : (slot + 1) * rows, :
                ].astype(F32)

            if plan.padded:
                pl.when(head < heads)(spread)
            else:
                spread()

    def narrow(t, carry):
        out_ref[t] = wide[pl.ds(pl.multiple_of(t * heads, 8), heads), :].astype(BF16)
        return carry

    lax.fori_loop(0, rows, narrow, 0, unroll=8)


def unpack(plan, items, me, backs):
    rows, heads, dim = plan.rows, plan.heads, plan.dim
    vmem_spec = pl.BlockSpec(memory_space=pltpu.VMEM)
    return pl.pallas_call(
        functools.partial(unpack_kernel, plan, items),
        in_specs=[pl.BlockSpec(memory_space=pltpu.SMEM)] + [vmem_spec] * len(backs),
        out_specs=vmem_spec,
        out_shape=jax.ShapeDtypeStruct((rows, heads, dim), BF16),
        scratch_shapes=[pltpu.VMEM((rows * heads, dim), F32)],
        compiler_params=params(),
        cost_estimate=cost(0, 4 << 20),
        name="unpack",
    )(me, *backs)


class Sender:
    def __init__(self, seq):
        self.seq, self.ended = seq, []

    def send(self, array, step, after=None, window=WINDOW):
        if after is not None:
            array, _ = lax.optimization_barrier((array, after))
        if len(self.ended) >= window:
            array, _ = lax.optimization_barrier((array, self.ended[-window]))
        got = lax.ppermute(array, "seq", [(d, d ^ (2 * step)) for d in range(self.seq)])
        self.ended.append(got)
        return got


def mixed(far, near):
    far = far[::-1]
    order, far, near = far[:2], far[2:], near[1:]
    while far or near:
        order += near[:1] + far[:1]
        near, far = near[1:], far[1:]
    return order


def body(seq, qkv, block_ids, counts):
    rows, heads, _, dim = qkv.shape
    plan = Plan(seq, heads, rows, dim, block_ids.shape[2], seq * block_ids.shape[0])
    scale = math.log2(math.e) / math.sqrt(dim)
    me = lax.axis_index("seq").astype(I32).reshape(1)
    by_kind = jnp.transpose(qkv, (0, 2, 1, 3))
    near, far, pieces = plan.near, plan.far, plan.pieces
    sender = Sender(seq)

    def work(piece, came, sent):
        if sent is not None:
            came, _ = lax.optimization_barrier((came, sent))
        mine = gather_keys(plan, piece, came)
        swapped = lax.ppermute(mine, "seq", [(d, d ^ 1) for d in range(seq)])
        return attend(plan, piece, me, came, mine, swapped, scale)

    far_items = [[(step, *piece) for step in far] for piece in pieces]
    near_items = [(step, 0, plan.per_chip) for step in near]
    rest_items = near_items + [item for items in far_items[1:] for item in items]
    packed = pack(plan, far_items[0], me, by_kind, block_ids, counts)
    rest = pack(plan, rest_items, me, by_kind, block_ids, counts)
    leaving = dict(zip(near, rest)) | dict(zip(far, packed))
    got = {step: sender.send(leaving[step], step) for step in mixed(far, near)}
    got[0] = rest[0]
    came = [got[step] for step in range(plan.chips)]
    items, backs = [], []

    def keep(piece, got):
        items.extend((step, *piece) for step in range(plan.chips))
        backs.extend(got[step] for step in range(plan.chips))

    if len(pieces) == 1:
        outs = work(pieces[0], came, None)
    else:
        last = rest[len(near) :]
        got = [sender.send(a, step) for a, step in zip(last[:LATE_A], far)]
        held = work(pieces[0], came, got[SEEN_A])
        got += [sender.send(a, step, held[0]) for a, step in zip(last[LATE_A:], far[LATE_A:])]
        came = came[: len(near)] + got
        got, order = {0: held[0]}, mixed(far, near)
        for step in order[:LATE_B]:
            got[step] = sender.send(held[step], step)
        outs = work(pieces[1], came, got[order[SEEN_B]])
        for step in order[LATE_B:]:
            got[step] = sender.send(held[step], step, outs[0])
        keep(pieces[0], got)
    got = {0: outs[0]}
    for step in mixed(far, near):
        got[step] = sender.send(outs[step], step, window=WINDOW_LAST)
    keep(pieces[-1], got)
    return unpack(plan, items, me, backs)


def solution(mesh):
    in_specs = (
        P(("rep", "seq"), None, None, None),
        P(("rep", "seq"), None, None),
        P(("rep", "seq"), None),
    )
    out_specs = P(("rep", "seq"), None, None)
    return jax.shard_map(
        functools.partial(body, mesh.shape["seq"]),
        mesh=mesh,
        in_specs=in_specs,
        out_specs=out_specs,
        check_vma=False,
    )
```
